128 devices in a mesh: row: 8 (over x_hi, y), col: 16 (over z, x_lo, core).
Axes of the slice: x: 4 (x_hi: 2, x_lo: 2; x = x_hi * 2 + x_lo), y: 4, z: 4, core: 2. Of those that a mesh axis runs over, the one named last changes fastest.
Arguments:
- tokens: bfloat16 [768, 8192], P('row', 'col'), may hold values from -6 to 6
- cotangent: bfloat16 [768, 8192], P('row', 'col'), may hold values from -6 to 6
- gate_weight: bfloat16 [8192, 14336], P('col', 'row'), may hold values from -0.09375 to 0.09375
- up_weight: bfloat16 [8192, 14336], P('col', 'row'), may hold values from -0.09375 to 0.09375
- down_weight: bfloat16 [14336, 8192], P('row', 'col'), may hold values from -0.0625 to 0.0625
- gate_mask: int32 [64, 112], P('col', 'row'), may hold values from 0 to 1, as said below
- up_mask: int32 [64, 112], P('col', 'row'), may hold values from 0 to 1, as said below
- down_mask: int32 [112, 64], P('row', 'col'), may hold values from 0 to 1, as said below
Outputs:
- layer_out: bfloat16 [768, 8192], P('row', 'col')
- input_grad: bfloat16 [768, 8192], P('row', 'col')
- gate_weight_grad: bfloat16 [8192, 14336], P('col', 'row')
- up_weight_grad: bfloat16 [8192, 14336], P('col', 'row')
- down_weight_grad: bfloat16 [14336, 8192], P('row', 'col')
The draws below stay inside these ranges and needn't reach their ends.
Inputs may be any that keep to these rules, and one draw needn't show every extreme that they name: `gate_mask`: 1 keeps a 128 x 128 block of the weight, 0 prunes it. `up_mask`: 1 keeps a 128 x 128 block of the weight, 0 prunes it. `down_mask`: 1 keeps a 128 x 128 block of the weight, 0 prunes it.
All inputs are finite; a program needn't handle non-finite values.
Results may differ from the reference program's by a relative error of at most 0.005.
Values may be sent and summed in bfloat16 or wider, within the bound.
No kernel may reach another device: no remote copies, remote signals or barrier semaphores. Data moves between devices by JAX's collectives and lax.ppermute only.
A program may use at most 128 MiB of HBM per device.

```python
import jax
import jax.numpy as jnp

D = 8192
FF = 14336
BLK = 128
TOKENS = 768


def uneven_blocks(key, block_rows, block_cols):
    levels = jax.random.randint(jax.random.fold_in(key, 101), (block_rows // 4, block_cols // 4), 1, 4)
    levels = jnp.repeat(jnp.repeat(levels, 4, axis=0), 4, axis=1)
    choose = jax.random.randint(jax.random.fold_in(key, 102), (block_rows, block_cols), 0, 4)
    return (choose < levels).astype(jnp.int32)


def draw_gate_mask(key, part):
    key = jax.random.fold_in(key, 11)
    return uneven_blocks(key, D // BLK, FF // BLK)


def draw_up_mask(key, part):
    key = jax.random.fold_in(key, 12)
    return uneven_blocks(key, D // BLK, FF // BLK)


def draw_down_mask(key, part):
    key = jax.random.fold_in(key, 13)
    return uneven_blocks(key, FF // BLK, D // BLK)


def block_levels(stream_key, shape, cuts, smallest, largest):
    factor_of, own = 1.0, jax.random.fold_in(stream_key, 6)
    for position, blocks in cuts:
        steps = jnp.exp(jax.random.uniform(jax.random.fold_in(own, position), (blocks,), jnp.float32, smallest / len(cuts), largest / len(cuts)))
        factor_of = factor_of * jnp.repeat(steps, shape[position] // blocks).reshape([-1 if axis == position else 1 for axis in range(len(shape))])
    return factor_of


def bell_draw(key, extent, scale, bound, shards=(), held_as=jnp.bfloat16):
    gain = block_levels(key, extent, shards, -0.22, 0.18) if shards else 1.0
    array = jax.random.normal(key, extent, jnp.float32) * scale * gain
    return jnp.minimum(jnp.maximum(array, -bound), bound).astype(held_as)


def setup_inputs(seed: int = 0) -> dict:
    seeds = jax.random.split(jax.random.key(seed), 9)
    tokens = bell_draw(seeds[0], (TOKENS, D), 1.0, 6.0, ((0, 8), (1, 16)))
    cotangent = bell_draw(seeds[1], (TOKENS, D), 1.0, 6.0, ((0, 8), (1, 16)))
    gate_weight = bell_draw(seeds[2], (D, FF), (D // 2) ** -0.5, 0.09375, ((0, 16), (1, 8)))
    up_weight = bell_draw(seeds[3], (D, FF), (D // 2) ** -0.5, 0.09375, ((0, 16), (1, 8)))
    down_weight = bell_draw(seeds[4], (FF, D), (FF // 2) ** -0.5, 0.0625, ((0, 8), (1, 16)))
    gate_mask = draw_gate_mask(jax.random.fold_in(seeds[8], 71), 0)
    up_mask = draw_up_mask(jax.random.fold_in(seeds[8], 71), 0)
    down_mask = draw_down_mask(jax.random.fold_in(seeds[8], 71), 0)
    return {"tokens": tokens, "cotangent": cotangent, "gate_weight": gate_weight, "up_weight": up_weight, "down_weight": down_weight, "gate_mask": gate_mask, "up_mask": up_mask, "down_mask": down_mask}


def expand(block_mask):
    return jnp.repeat(jnp.repeat(block_mask, BLK, axis=0), BLK, axis=1)


def pointwise(gate_proj, up_proj, hidden_grad):
    sigmoid_gate = jax.nn.sigmoid(gate_proj)
    silu_gate = gate_proj * sigmoid_gate
    hidden = (silu_gate * up_proj).astype(jnp.bfloat16)
    gate_grad = (hidden_grad * up_proj * sigmoid_gate * (1.0 + gate_proj * (1.0 - sigmoid_gate))).astype(jnp.bfloat16)
    up_grad = (hidden_grad * silu_gate).astype(jnp.bfloat16)
    return hidden, gate_grad, up_grad


def reference(tokens, cotangent, gate_weight, up_weight, down_weight, gate_mask, up_mask, down_mask):
    gate_full = expand(gate_mask)
    up_full = expand(up_mask)
    down_full = expand(down_mask)
    gate_eff = gate_weight * gate_full.astype(gate_weight.dtype)
    up_eff = up_weight * up_full.astype(up_weight.dtype)
    down_eff = down_weight * down_full.astype(down_weight.dtype)
    gate_proj = jnp.dot(tokens, gate_eff, preferred_element_type=jnp.float32)
    up_proj = jnp.dot(tokens, up_eff, preferred_element_type=jnp.float32)
    hidden_grad = jnp.dot(cotangent, down_eff.T, preferred_element_type=jnp.float32)
    hidden, gate_grad, up_grad = pointwise(gate_proj, up_proj, hidden_grad)
    layer_out = jnp.dot(hidden, down_eff, preferred_element_type=jnp.float32).astype(jnp.bfloat16)
    input_sum = jnp.dot(gate_grad, gate_eff.T, preferred_element_type=jnp.float32) + jnp.dot(up_grad, up_eff.T, preferred_element_type=jnp.float32)
    input_grad = input_sum.astype(jnp.bfloat16)
    gate_weight_grad = (jnp.dot(tokens.T, gate_grad, preferred_element_type=jnp.float32) * gate_full.astype(jnp.float32)).astype(jnp.bfloat16)
    up_weight_grad = (jnp.dot(tokens.T, up_grad, preferred_element_type=jnp.float32) * up_full.astype(jnp.float32)).astype(jnp.bfloat16)
    down_weight_grad = (jnp.dot(hidden.T, cotangent, preferred_element_type=jnp.float32) * down_full.astype(jnp.float32)).astype(jnp.bfloat16)
    return (layer_out, input_grad, gate_weight_grad, up_weight_grad, down_weight_grad)
```

```python
import jax
import jax.numpy as jnp
from jax import lax
from jax.sharding import PartitionSpec as P

BLK = 128
BF = jnp.bfloat16
F32 = jnp.float32

GRAY = ((0, 0), (1, 0), (1, 1), (0, 1))
RING = {bits: pos for pos, bits in enumerate(GRAY)}
AXIS = {"A": 0, "B": 1, "X": 2}
ORDERS = ("ABX", "BXA", "XAB")


def flip_ring(pos, dim):
    bits = list(GRAY[pos])
    bits[dim] ^= 1
    return RING[tuple(bits)]


def col_perm(dim):
    pairs = []
    for i in range(16):
        z, x, c = i // 4, (i // 2) % 2, i % 2
        if dim in "AB":
            z = flip_ring(z, AXIS[dim])
        elif dim == "X":
            x ^= 1
        else:
            c ^= 1
        pairs.append((i, (z * 2 + x) * 2 + c))
    return pairs


def row_perm(dim):
    pairs = []
    for i in range(8):
        x, y = i // 4, i % 4
        if dim in "AB":
            y = flip_ring(y, AXIS[dim])
        else:
            x ^= 1
        pairs.append((i, x * 4 + y))
    return pairs


def swap_col(value, dim):
    return lax.ppermute(value, "col", col_perm(dim))


def swap_row(value, dim):
    return lax.ppermute(value, "row", row_perm(dim))


def ring_bits(pos):
    return ((pos == 1) | (pos == 2)).astype(jnp.int32), (pos >= 2).astype(jnp.int32)


def place(row):
    bit_a, bit_b = ring_bits(row % 4)
    return bit_a * 4 + bit_b * 2 + row // 4


def take(value, axis, index):
    return lax.dynamic_index_in_dim(value, index, axis, keepdims=True)


def halve(parts, bits, swap, types):
    parts = list(parts)
    for step in range(3):
        got = []
        for i, part in enumerate(parts):
            dim = ORDERS[i][step]
            got.append(swap(take(part, AXIS[dim], 1 - bits[dim]).astype(types[step]), dim))
        for i, part in enumerate(parts):
            dim = ORDERS[i][step]
            parts[i] = take(part, AXIS[dim], bits[dim]) + got[i].astype(F32)
    return [part[0, 0, 0] for part in parts]


def double(parts, bits, swap):
    rows = parts[0].shape[0]
    parts = [part[None, None, None] for part in parts]
    for step in range(3):
        got = [swap(part, ORDERS[i][step]) for i, part in enumerate(parts)]
        for i, part in enumerate(parts):
            dim = ORDERS[i][step]
            first = jnp.where(bits[dim] == 0, part, got[i])
            second = jnp.where(bits[dim] == 0, got[i], part)
            parts[i] = jnp.concatenate([first, second], axis=AXIS[dim])
    return [part.reshape(8 * rows, -1) for part in parts]


def pointwise(gate_proj, up_proj, hidden_grad):
    sigmoid_gate = jax.nn.sigmoid(gate_proj)
    silu_gate = gate_proj * sigmoid_gate
    hidden = (silu_gate * up_proj).astype(BF)
    gate_grad = (
        hidden_grad * up_proj * sigmoid_gate * (1.0 + gate_proj * (1.0 - sigmoid_gate))
    ).astype(BF)
    up_grad = (hidden_grad * silu_gate).astype(BF)
    return hidden, gate_grad, up_grad


def expand(block_mask):
    return jnp.repeat(jnp.repeat(block_mask, BLK, axis=0), BLK, axis=1)


def dot(a, b, dims):
    return lax.dot_general(a, b, (dims, ((), ())), preferred_element_type=F32)


NN = ((1,), (0,))
NT = ((1,), (1,))
TN = ((0,), (0,))


def per_device(
    tokens, cotangent, gate_weight, up_weight, down_weight, gate_mask, up_mask, down_mask
):
    col, row = lax.axis_index("col"), lax.axis_index("row")
    core = col % 2
    bit_a, bit_b = ring_bits(col // 4)
    col_bits = {"A": bit_a, "B": bit_b, "X": (col // 2) % 2}
    bit_a, bit_b = ring_bits(row % 4)
    row_bits = {"A": bit_a, "B": bit_b, "X": row // 4}

    gate_full = expand(gate_mask).astype(BF)
    up_full = expand(up_mask).astype(BF)
    down_full = expand(down_mask).astype(BF)
    gate_eff = gate_weight * gate_full
    up_eff = up_weight * up_full
    down_eff = down_weight * down_full
    half = gate_eff.shape[1] // 2
    width = tokens.shape[1]

    def trade(weight, axis):
        kept = lax.dynamic_slice_in_dim(weight, core * half, half, axis)
        sent = lax.dynamic_slice_in_dim(weight, (1 - core) * half, half, axis)
        return jnp.concatenate([kept, swap_col(sent, "C")], axis=1 - axis)

    both = jnp.concatenate([tokens, cotangent], axis=1)
    row_of = [swap_to(both, k) for k in range(1, 8)]
    panel = jnp.zeros((8,) + both.shape, BF)
    panel = lax.dynamic_update_index_in_dim(panel, both, place(row), 0)
    for k in range(1, 8):
        panel = lax.dynamic_update_index_in_dim(panel, row_of[k - 1], place(row ^ k), 0)
    panel = panel.reshape(-1, 2 * width)
    other = swap_col(panel, "C")
    token_panel = jnp.concatenate([panel[:, :width], other[:, :width]], axis=1)
    grad_panel = jnp.concatenate([panel[:, width:], other[:, width:]], axis=1)

    gate_eff = trade(gate_eff, 1)
    up_eff = trade(up_eff, 1)
    down_eff = trade(down_eff, 0)

    gate_part = dot(token_panel, gate_eff, NN)
    up_part = dot(token_panel, up_eff, NN)
    hidden_part = dot(grad_panel, down_eff, NT)
    cube = (2, 2, 2, gate_part.shape[0] // 8, half)
    sums = halve(
        [part.reshape(cube) for part in (gate_part, up_part, hidden_part)],
        col_bits,
        swap_col,
        (BF, BF, F32),
    )
    hidden_all, gate_all, up_all = double(pointwise(*sums), col_bits, swap_col)

    out_term = dot(hidden_all, down_eff, NN)
    input_term = dot(gate_all, gate_eff, NT) + dot(up_all, up_eff, NT)
    out_term = out_term[:, :width] + swap_col(out_term[:, width:].astype(BF), "C").astype(F32)
    input_term = input_term[:, :width] + swap_col(input_term[:, width:].astype(BF), "C").astype(F32)
    terms = jnp.concatenate([out_term, input_term], axis=1)
    cuts = (0, 3 * width // 4, 6 * width // 4, 2 * width)
    cube = (2, 2, 2, terms.shape[0] // 8)
    sums = halve(
        [terms[:, a:b].reshape(cube + (b - a,)) for a, b in zip(cuts, cuts[1:])],
        row_bits,
        swap_row,
        (BF, BF, F32),
    )
    sums = jnp.concatenate(sums, axis=1)

    def give_back(grad, axis):
        kept = lax.slice_in_dim(grad, 0, width, axis=1 - axis)
        got = swap_col(lax.slice_in_dim(grad, width, 2 * width, axis=1 - axis), "C")
        first = jnp.where(core == 0, kept, got)
        second = jnp.where(core == 0, got, kept)
        return jnp.concatenate([first, second], axis=axis)

    gate_weight_grad = give_back(dot(token_panel, gate_all, TN).astype(BF), 1) * gate_full
    up_weight_grad = give_back(dot(token_panel, up_all, TN).astype(BF), 1) * up_full
    down_weight_grad = give_back(dot(hidden_all, grad_panel, TN).astype(BF), 0) * down_full
    return (
        sums[:, :width].astype(BF),
        sums[:, width:].astype(BF),
        gate_weight_grad,
        up_weight_grad,
        down_weight_grad,
    )


def swap_to(value, k):
    return lax.ppermute(value, "row", [(i, i ^ k) for i in range(8)])


def solution(mesh):
    placed = (
        P("row", "col"),
        P("row", "col"),
        P("col", "row"),
        P("col", "row"),
        P("row", "col"),
        P("col", "row"),
        P("col", "row"),
        P("row", "col"),
    )
    return jax.shard_map(
        per_device,
        mesh=mesh,
        in_specs=placed,
        out_specs=(
            P("row", "col"),
            P("row", "col"),
            P("col", "row"),
            P("col", "row"),
            P("row", "col"),
        ),
        check_vma=False,
    )
```

```python
import functools

import jax
import jax.numpy as jnp
import numpy as np
from jax import lax
from jax.experimental import pallas as pl
from jax.experimental.pallas import tpu as pltpu
from jax.sharding import PartitionSpec as P

BLK = 128
BF = jnp.bfloat16
F32 = jnp.float32

GRAY = ((0, 0), (1, 0), (1, 1), (0, 1))
RING = {bits: pos for pos, bits in enumerate(GRAY)}
MASK = {"A": 4, "B": 2, "X": 1}
ORDERS = ("ABX", "BXA", "XAB")
NEAR = ("", "A", "B", "X")
FAR = ("AB", "AX", "BX", "ABX")


def flip_ring(pos, dims):
    bit_a, bit_b = GRAY[pos]
    return RING[(bit_a ^ ("A" in dims), bit_b ^ ("B" in dims))]


def flip_col(i, dims):
    z, x, c = i // 4, (i // 2) % 2, i % 2
    return (flip_ring(z, dims) * 2 + (x ^ ("X" in dims))) * 2 + c


def flip_row(i, dims):
    return (i // 4 ^ ("X" in dims)) * 4 + flip_ring(i % 4, dims)


def swap_core(value):
    return lax.ppermute(value, "col", [(i, i ^ 1) for i in range(16)])


def swap_cube(parts, step):
    return [
        lax.ppermute(part, "col", [(i, flip_col(i, order[step])) for i in range(16)])
        for part, order in zip(parts, ORDERS)
    ]


def swap_row(value, dims):
    return lax.ppermute(value, "row", [(i, flip_row(i, dims)) for i in range(8)])


def make_table():
    rows = []
    for i in range(16):
        bit_a, bit_b = GRAY[i // 4]
        own = bit_a * 4 + bit_b * 2 + (i // 2) % 2
        row = [i % 2]
        for order in ORDERS:
            for place in range(8):
                bits = (place >> 2, (place >> 1) & 1, place & 1)
                row.append(own ^ sum(MASK[d] * b for d, b in zip(order, bits)))
        rows.append(row)
    return np.array(rows, np.int32)


def dot(a, b, dims=((1,), (0,))):
    return lax.dot_general(a, b, (dims, ((), ())), preferred_element_type=F32)


NT = ((1,), (1,))
PARAMS = pltpu.CompilerParams(vmem_limit_bytes=24 * 1024 * 1024)


def call(kernel, prefetch, grid, in_specs, out_specs, out_shape, scratch=(), flops=0, size=0, **more):
    return pl.pallas_call(
        kernel,
        grid_spec=pltpu.PrefetchScalarGridSpec(
            num_scalar_prefetch=prefetch,
            grid=grid,
            in_specs=in_specs,
            out_specs=out_specs,
            scratch_shapes=list(scratch),
        ),
        out_shape=out_shape,
        compiler_params=PARAMS,
        cost_estimate=pl.CostEstimate(flops=flops, bytes_accessed=size, transcendentals=0),
        **more,
    )


def shape(dims, dtype):
    return jax.ShapeDtypeStruct(dims, dtype)


def whole(dims):
    return pl.BlockSpec(dims, lambda *_: (0,) * len(dims))


def times(block, keep):
    return (block.astype(F32) * keep.astype(F32)).astype(BF)


def prepare_kernel(info, gm, um, dm, gk, gs, uk, us, dk, ds, gu_keep, gu_send, d_keep, d_send):
    j = pl.program_id(0)
    blocks, halves = gk.shape[0] // BLK, pl.num_programs(0)
    for side, (g, u, d, gu_out, d_out) in enumerate(
        ((gk, uk, dk, gu_keep, d_keep), (gs, us, ds, gu_send, d_send))
    ):
        core = info[0] if side == 0 else 1 - info[0]
        at = core * halves + j
        for f in range(blocks):
            rows = slice(f * BLK, (f + 1) * BLK)
            gu_out[0, rows, :] = times(g[rows, :], gm[f, at])
            gu_out[1, rows, :] = times(u[rows, :], um[f, at])
            d_out[:, rows] = times(d[:, rows], dm[at, f])


def prepare(info, gm, um, dm, gate_weight, up_weight, down_weight):
    width, hidden = gate_weight.shape
    half, n = hidden // 2, hidden // 2 // BLK

    def wide(side):
        return pl.BlockSpec(
            (width, BLK), lambda j, info, *_: (0, (info[0] if side == 0 else 1 - info[0]) * n + j)
        )

    def tall(side):
        return pl.BlockSpec(
            (BLK, width), lambda j, info, *_: ((info[0] if side == 0 else 1 - info[0]) * n + j, 0)
        )

    gu_spec = pl.BlockSpec((2, width, BLK), lambda j, *_: (0, 0, j))
    d_spec = pl.BlockSpec((BLK, width), lambda j, *_: (j, 0))
    return call(
        prepare_kernel,
        4,
        (n,),
        [wide(0), wide(1), wide(0), wide(1), tall(0), tall(1)],
        [gu_spec, gu_spec, d_spec, d_spec],
        [shape((2, width, half), BF)] * 2 + [shape((half, width), BF)] * 2,
        size=12 * width * hidden,
    )(info, gm, um, dm, gate_weight, gate_weight, up_weight, up_weight, down_weight, down_weight)


def project_kernel(info, own_a, own_b, oth_a, oth_b, gu_own, gu_oth, d_own, d_oth, *refs, base):
    outs, panel = refs[:3], refs[3]
    rows, width = own_a.shape[0], own_a.shape[1] // 2
    r = rows // 4
    for q in range(3):
        cols = slice(0, width) if q < 2 else slice(width, 2 * width)
        for k in range(4):
            at = info[1 + 8 * q + base + k]
            to = slice(k * r, (k + 1) * r)
            row = pl.ds(pl.multiple_of((at % 4) * r, 16), r)

            @pl.when(at < 4)
            def _():
                panel[q, to, :width] = own_a[row, cols]
                panel[q, to, width:] = oth_a[row, cols]

            @pl.when(at >= 4)
            def _():
                panel[q, to, :width] = own_b[row, cols]
                panel[q, to, width:] = oth_b[row, cols]

    for q in range(2):
        w = jnp.concatenate([gu_own[q], gu_oth[q]], axis=0)
        outs[q][...] = dot(panel[q], w).astype(outs[q].dtype)
    w = jnp.concatenate([d_own[...], d_oth[...]], axis=1)
    outs[2][...] = dot(panel[2], w, NT).astype(outs[2].dtype)


def project(info, panels, weights, base, kind):
    rows, width = panels[0].shape[0], panels[0].shape[1] // 2
    count = weights[2].shape[0]
    return call(
        functools.partial(project_kernel, base=base),
        1,
        (1,),
        [whole(v.shape) for v in (*panels, *weights)],
        [whole((rows, count))] * 3,
        [shape((rows, count), kind)] * 3,
        [pltpu.VMEM((3, rows, 2 * width), BF)],
        flops=12 * rows * width * count,
        size=12 * rows * count + 12 * width * count + 8 * rows * width,
    )(info, *panels, *weights)


def pointwise(gate_proj, up_proj, hidden_grad):
    sigmoid_gate = jax.nn.sigmoid(gate_proj)
    silu_gate = gate_proj * sigmoid_gate
    hidden = (silu_gate * up_proj).astype(BF)
    gate_grad = (
        hidden_grad * up_proj * sigmoid_gate * (1.0 + gate_proj * (1.0 - sigmoid_gate))
    ).astype(BF)
    up_grad = (hidden_grad * silu_gate).astype(BF)
    return hidden, gate_grad, up_grad


def exchange(sends, keeps):
    for step in range(3):
        got = swap_cube(sends, step)
        sums = [keep + g.astype(F32) for keep, g in zip(keeps, got)]
        if step < 2:
            n = sums[0].shape[0] // 2
            keeps = [v[:n] for v in sums]
            sends = [v[n:].astype(BF) for v in sums]
    hidden, gate_grad, up_grad = pointwise(*sums)
    parts = [gate_grad, up_grad, hidden]
    for step in (2, 1, 0):
        got = swap_cube(parts, step)
        if step == 0:
            return parts + got
        parts = [jnp.concatenate([part, g], axis=0) for part, g in zip(parts, got)]


def gather_kernel(info, *refs):
    halves, acts = (refs[:3], refs[3:6]), refs[6]
    r = acts.shape[0] // 8
    n = acts.shape[1] // 3
    for q in range(3):
        for k in range(8):
            at = pl.ds(pl.multiple_of(info[1 + 8 * q + k] * r, 16), r)
            acts[at, q * n : (q + 1) * n] = halves[k // 4][q][k % 4 * r : (k % 4 + 1) * r, :]


def gather(info, pieces):
    rows, count = 2 * pieces[0].shape[0], 3 * pieces[0].shape[1]
    return call(
        gather_kernel,
        1,
        (1,),
        [whole(v.shape) for v in pieces],
        whole((rows, count)),
        shape((rows, count), BF),
        size=4 * rows * count,
    )(info, *pieces)


def backward_kernel(acts, gu, d, terms):
    n = acts.shape[1] // 3
    terms[0] = dot(acts[:, 2 * n :], d[...]).astype(terms.dtype)
    inp = dot(acts[:, :n], gu[0], NT) + dot(acts[:, n : 2 * n], gu[1], NT)
    terms[1] = inp.astype(terms.dtype)


def backward(acts, gu, d, kind):
    rows, count, width = acts.shape[0], acts.shape[1], d.shape[1]
    step = 2 * BLK
    return call(
        backward_kernel,
        0,
        (width // step,),
        [
            whole(acts.shape),
            pl.BlockSpec((2, step, d.shape[0]), lambda i: (0, i, 0)),
            pl.BlockSpec((d.shape[0], step), lambda i: (0, i)),
        ],
        pl.BlockSpec((2, rows, step), lambda i: (0, 0, i)),
        shape((2, rows, width), kind),
        flops=2 * rows * width * count,
        size=2 * width * count + 2 * rows * count,
    )(acts, gu, d)


def grads_kernel(info, gm, um, dm, own_a, own_b, gg, ug, hid, *refs, mine):
    outs, tok_t, cot = refs[-5:-2], refs[-2], refs[-1]
    j = pl.program_id(0)
    rows, width = own_a.shape[0], own_a.shape[1] // 2

    @pl.when(j == 0)
    def _():
        tok_t[:, :rows] = own_a[:, :width].T
        tok_t[:, rows:] = own_b[:, :width].T
        cot[:rows, :] = own_a[:, width:]
        cot[rows:, :] = own_b[:, width:]

    gu = dot(tok_t[...], jnp.concatenate([gg[...], ug[...]], axis=1))
    d = dot(hid[...].T, cot[...])
    at = (info[0] if mine else 1 - info[0]) * pl.num_programs(0) + j
    g_out, u_out, d_out = outs
    for f in range(width // BLK):
        block = slice(f * BLK, (f + 1) * BLK)
        g_out[block, :] = (gu[block, :BLK] * gm[f, at].astype(F32)).astype(BF)
        u_out[block, :] = (gu[block, BLK:] * um[f, at].astype(F32)).astype(BF)
        d_out[:, block] = (d[:, block] * dm[at, f].astype(F32)).astype(BF)


def grads(info, masks, panels, acts, into=()):
    rows, width = panels[0].shape[0], panels[0].shape[1] // 2
    n = acts.shape[1] // 3 // BLK
    hidden = 2 * n * BLK

    def half(info):
        return (1 - info[0] if into else info[0]) * n

    wide = pl.BlockSpec((width, BLK), lambda j, info, *_: (0, half(info) + j))
    tall = pl.BlockSpec((BLK, width), lambda j, info, *_: (half(info) + j, 0))
    wide_shape = shape((width, hidden), BF)
    return call(
        functools.partial(grads_kernel, mine=not into),
        4,
        (n,),
        [whole(v.shape) for v in panels]
        + [
            pl.BlockSpec((2 * rows, BLK), lambda j, *_, q=q: (0, q * n + j))
            for q in range(3)
        ]
        + [pl.BlockSpec(memory_space=pl.ANY)] * len(into),
        [wide, wide, tall],
        [wide_shape, wide_shape, shape((hidden, width), BF)],
        [pltpu.VMEM((width, 2 * rows), BF), pltpu.VMEM((2 * rows, width), BF)],
        flops=6 * rows * width * hidden,
        size=3 * width * hidden + 6 * rows * hidden,
        **({"input_output_aliases": {9: 0, 10: 1, 11: 2}} if into else {}),
    )(info, *masks, *panels, acts, acts, acts, *into)


def per_device(
    tokens, cotangent, gate_weight, up_weight, down_weight, gate_mask, up_mask, down_mask
):
    masks = (gate_mask, up_mask, down_mask)
    info = lax.dynamic_index_in_dim(jnp.asarray(make_table()), lax.axis_index("col"), 0, keepdims=False)
    names = NEAR[1:] + FAR
    both = jnp.concatenate([tokens, cotangent], axis=1)
    got = [swap_row(both, d) for d in names[:5]]
    gu_own, gu_send, d_own, d_send = prepare(info, *masks, gate_weight, up_weight, down_weight)
    late, gu_send, d_send, *got = lax.optimization_barrier((both, gu_send, d_send, *got))
    gu_oth, d_oth = swap_core(gu_send), swap_core(d_send)
    got += [swap_row(late, d) for d in names[5:]]
    own = [jnp.concatenate(blocks, axis=0) for blocks in ([both, *got[:3]], got[3:])]
    oth = [swap_core(panel) for panel in own]

    panels, weights = (*own, *oth), (gu_own, gu_oth, d_own, d_oth)
    sends = project(info, panels, weights, 4, BF)
    keeps = project(info, panels, weights, 0, F32)
    acts = gather(info, exchange(sends, keeps))

    got = swap_core(backward(acts, gu_oth, d_oth, F32))
    part = backward(acts, gu_own, d_own, F32) + got
    parts = jnp.split(part, 8, axis=1)
    acts, *blocks = lax.optimization_barrier([acts] + [p.astype(BF) for p in parts[1:]])
    got = [swap_row(block, d) for block, d in zip(blocks[:4], names[:4])]
    sib = swap_core(acts)
    partial = grads(info, masks, own, acts)
    sib, *rest = lax.optimization_barrier([sib] + got + blocks[4:])
    got = rest[:4] + [swap_row(block, d) for block, d in zip(rest[4:], names[4:])]
    weight_grads = grads(info, masks, own, sib, partial)
    total = parts[0]
    for block in got:
        total = total + block.astype(F32)
    total = total.astype(BF)
    return (total[0], total[1], *weight_grads)


def solution(mesh):
    placed = (
        P("row", "col"),
        P("row", "col"),
        P("col", "row"),
        P("col", "row"),
        P("row", "col"),
        P("col", "row"),
        P("col", "row"),
        P("row", "col"),
    )
    return jax.shard_map(
        per_device,
        mesh=mesh,
        in_specs=placed,
        out_specs=(
            P("row", "col"),
            P("row", "col"),
            P("col", "row"),
            P("col", "row"),
            P("row", "col"),
        ),
        check_vma=False,
    )
```

```python
import functools

import jax
import jax.numpy as jnp
import numpy as np
from jax import lax
from jax.experimental import pallas as pl
from jax.experimental.pallas import tpu as pltpu
from jax.sharding import PartitionSpec as P

BLK = 128
BF = jnp.bfloat16
F32 = jnp.float32

GRAY = ((0, 0), (1, 0), (1, 1), (0, 1))
RING = {bits: pos for pos, bits in enumerate(GRAY)}
MASK = {"A": 4, "B": 2, "X": 1}
ORDERS = ("ABX", "BXA", "XAB")

def flip_ring(pos, dims):
    bit_a, bit_b = GRAY[pos]
    return RING[(bit_a ^ ("A" in dims), bit_b ^ ("B" in dims))]


def flip_col(i, dims):
    z, x, c = i // 4, (i // 2) % 2, i % 2
    return (flip_ring(z, dims) * 2 + (x ^ ("X" in dims))) * 2 + c


def flip_row(i, dims):
    return (i // 4 ^ ("X" in dims)) * 4 + flip_ring(i % 4, dims)


def swap_core(value):
    return lax.ppermute(value, "col", [(i, i ^ 1) for i in range(16)])


def swap_cube(parts, step):
    return [
        lax.ppermute(part, "col", [(i, flip_col(i, order[step])) for i in range(16)])
        for part, order in zip(parts, ORDERS)
    ]


def swap_row(value, dims):
    return lax.ppermute(value, "row", [(i, flip_row(i, dims)) for i in range(8)])


def make_table():
    rows = []
    for i in range(16):
        bit_a, bit_b = GRAY[i // 4]
        own = bit_a * 4 + bit_b * 2 + (i // 2) % 2
        row = [i % 2]
        for order in ORDERS:
            for place in range(8):
                bits = (place >> 2, (place >> 1) & 1, place & 1)
                row.append(own ^ sum(MASK[d] * b for d, b in zip(order, bits)))
        rows.append(row)
    return np.array(rows, np.int32)


def dot(a, b, dims=((1,), (0,))):
    return lax.dot_general(a, b, (dims, ((), ())), preferred_element_type=F32)


NT = ((1,), (1,))
PARAMS = pltpu.CompilerParams(vmem_limit_bytes=24 * 1024 * 1024)


def call(kernel, prefetch, grid, in_specs, out_specs, out_shape, scratch=(), flops=0, size=0, params=PARAMS, **more):
    return pl.pallas_call(
        kernel,
        grid_spec=pltpu.PrefetchScalarGridSpec(
            num_scalar_prefetch=prefetch,
            grid=grid,
            in_specs=in_specs,
            out_specs=out_specs,
            scratch_shapes=list(scratch),
        ),
        out_shape=out_shape,
        compiler_params=params,
        cost_estimate=pl.CostEstimate(flops=flops, bytes_accessed=size, transcendentals=0),
        **more,
    )


def shape(dims, dtype):
    return jax.ShapeDtypeStruct(dims, dtype)


def whole(dims):
    return pl.BlockSpec(dims, lambda *_: (0,) * len(dims))


def times(block, keep):
    return (block.astype(F32) * keep.astype(F32)).astype(BF)


def prepare_kernel(info, gm, um, dm, gk, gs, uk, us, dk, ds, gu_keep, gu_send, d_keep, d_send):
    f = pl.program_id(0)
    n = gk.shape[1] // BLK
    for side, (g, u, d, gu_out, d_out) in enumerate(
        ((gk, uk, dk, gu_keep, d_keep), (gs, us, ds, gu_send, d_send))
    ):
        first = (info[0] if side == 0 else 1 - info[0]) * n
        for j in range(n):
            at = slice(j * BLK, (j + 1) * BLK)
            gu_out[0, :, at] = times(g[:, at], gm[f, first + j])
            gu_out[1, :, at] = times(u[:, at], um[f, first + j])
            d_out[at, :] = times(d[at, :], dm[first + j, f])


def prepare(info, gm, um, dm, gate_weight, up_weight, down_weight):
    width, hidden = gate_weight.shape
    half = hidden // 2

    def wide(side):
        return pl.BlockSpec((BLK, half), lambda f, info, *_: (f, info[0] if side == 0 else 1 - info[0]))

    def tall(side):
        return pl.BlockSpec((half, BLK), lambda f, info, *_: (info[0] if side == 0 else 1 - info[0], f))

    gu_spec = pl.BlockSpec((2, BLK, half), lambda f, *_: (0, f, 0))
    d_spec = pl.BlockSpec((half, BLK), lambda f, *_: (0, f))
    return call(
        prepare_kernel,
        4,
        (width // BLK,),
        [wide(0), wide(1), wide(0), wide(1), tall(0), tall(1)],
        [gu_spec, gu_spec, d_spec, d_spec],
        [shape((2, width, half), BF)] * 2 + [shape((half, width), BF)] * 2,
        size=12 * width * hidden,
        params=pltpu.CompilerParams(vmem_limit_bytes=52 * 1024 * 1024),
    )(info, gm, um, dm, gate_weight, gate_weight, up_weight, up_weight, down_weight, down_weight)


def project_kernel(info, own_a, own_b, oth_a, oth_b, *refs, base, parts):
    outs, panel = refs[-1 - len(parts) : -1], refs[-1]
    rows, width = own_a.shape[0], own_a.shape[1] // 2
    r = rows // 4
    for n, q in enumerate(parts):
        cols = slice(0, width) if q < 2 else slice(width, 2 * width)
        for k in range(4):
            at = info[1 + 8 * q + base + k]
            to = slice(k * r, (k + 1) * r)
            row = pl.ds(pl.multiple_of((at % 4) * r, 16), r)

            @pl.when(at < 4)
            def _():
                panel[n, to, :width] = own_a[row, cols]
                panel[n, to, width:] = oth_a[row, cols]

            @pl.when(at >= 4)
            def _():
                panel[n, to, :width] = own_b[row, cols]
                panel[n, to, width:] = oth_b[row, cols]

    for n, q in enumerate(parts):
        w_own, w_oth = refs[2 * n], refs[2 * n + 1]
        if q < 2:
            w, dims = jnp.concatenate([w_own[0], w_oth[0]], axis=0), ((1,), (0,))
        else:
            w, dims = jnp.concatenate([w_own[...], w_oth[...]], axis=1), NT
        outs[n][...] = dot(panel[n], w, dims).astype(outs[n].dtype)


def project(info, panels, weights, base, parts, kind):
    rows, width = panels[0].shape[0], panels[0].shape[1] // 2
    gu_own, gu_oth, d_own, d_oth = weights
    count = d_own.shape[0]
    args, specs = [], []
    for q in parts:
        if q < 2:
            args += [gu_own, gu_oth]
            specs += [pl.BlockSpec((1, width, count), lambda i, *_, q=q: (q, 0, 0))] * 2
        else:
            args += [d_own, d_oth]
            specs += [whole(d_own.shape)] * 2
    return call(
        functools.partial(project_kernel, base=base, parts=parts),
        1,
        (1,),
        [whole(v.shape) for v in panels] + specs,
        [whole((rows, count))] * len(parts),
        [shape((rows, count), kind)] * len(parts),
        [pltpu.VMEM((len(parts), rows, 2 * width), BF)],
        flops=4 * rows * width * count * len(parts),
        size=4 * (rows + width) * count * len(parts) + 8 * rows * width,
    )(info, *panels, *args)


def pointwise(gate_proj, up_proj, hidden_grad):
    sigmoid_gate = jax.nn.sigmoid(gate_proj)
    silu_gate = gate_proj * sigmoid_gate
    hidden = (silu_gate * up_proj).astype(BF)
    gate_grad = (
        hidden_grad * up_proj * sigmoid_gate * (1.0 + gate_proj * (1.0 - sigmoid_gate))
    ).astype(BF)
    up_grad = (hidden_grad * silu_gate).astype(BF)
    return hidden, gate_grad, up_grad


def exchange(sends, keeps):
    for step in range(3):
        got = swap_cube(sends, step)
        sums = [keep + g.astype(F32) for keep, g in zip(keeps, got)]
        if step < 2:
            n = sums[0].shape[0] // 2
            keeps = [v[:n] for v in sums]
            sends = [v[n:].astype(BF) for v in sums]
    hidden, gate_grad, up_grad = pointwise(*sums)
    parts = [gate_grad, up_grad, hidden]
    for step in (2, 1, 0):
        got = swap_cube(parts, step)
        if step == 0:
            return parts + got
        parts = [jnp.concatenate([part, g], axis=0) for part, g in zip(parts, got)]


def gather_kernel(info, *refs):
    halves, acts = (refs[:3], refs[3:6]), refs[6]
    r = acts.shape[0] // 8
    n = acts.shape[1] // 3
    for q in range(3):
        for k in range(8):
            at = pl.ds(pl.multiple_of(info[1 + 8 * q + k] * r, 16), r)
            acts[at, q * n : (q + 1) * n] = halves[k // 4][q][k % 4 * r : (k % 4 + 1) * r, :]


def gather(info, pieces):
    rows, count = 2 * pieces[0].shape[0], 3 * pieces[0].shape[1]
    return call(
        gather_kernel,
        1,
        (1,),
        [whole(v.shape) for v in pieces],
        whole((rows, count)),
        shape((rows, count), BF),
        size=4 * rows * count,
    )(info, *pieces)


def backward_kernel(acts, gu, d, terms):
    n = acts.shape[1] // 3
    terms[0] = dot(acts[:, 2 * n :], d[...]).astype(terms.dtype)
    inp = dot(acts[:, :n], gu[0], NT) + dot(acts[:, n : 2 * n], gu[1], NT)
    terms[1] = inp.astype(terms.dtype)


def backward(acts, gu, d, kind):
    rows, count, width = acts.shape[0], acts.shape[1], d.shape[1]
    step = 2 * BLK
    return call(
        backward_kernel,
        0,
        (width // step,),
        [
            whole(acts.shape),
            pl.BlockSpec((2, step, d.shape[0]), lambda i: (0, i, 0)),
            pl.BlockSpec((d.shape[0], step), lambda i: (0, i)),
        ],
        pl.BlockSpec((2, rows, step), lambda i: (0, 0, i)),
        shape((2, rows, width), kind),
        flops=2 * rows * width * count,
        size=2 * width * count + 2 * rows * count,
    )(acts, gu, d)


def grads_kernel(info, gm, um, dm, own_a, own_b, gg, ug, hid, *refs, mine):
    outs, tok_t, cot = refs[-5:-2], refs[-2], refs[-1]
    j = pl.program_id(0)
    rows, width = own_a.shape[0], own_a.shape[1] // 2

    @pl.when(j == 0)
    def _():
        tok_t[:, :rows] = own_a[:, :width].T
        tok_t[:, rows:] = own_b[:, :width].T
        cot[:rows, :] = own_a[:, width:]
        cot[rows:, :] = own_b[:, width:]

    gu = dot(tok_t[...], jnp.concatenate([gg[...], ug[...]], axis=1))
    d = dot(hid[...].T, cot[...])
    at = (info[0] if mine else 1 - info[0]) * pl.num_programs(0) + j
    g_out, u_out, d_out = outs
    for f in range(width // BLK):
        block = slice(f * BLK, (f + 1) * BLK)
        g_out[block, :] = (gu[block, :BLK] * gm[f, at].astype(F32)).astype(BF)
        u_out[block, :] = (gu[block, BLK:] * um[f, at].astype(F32)).astype(BF)
        d_out[:, block] = (d[:, block] * dm[at, f].astype(F32)).astype(BF)


def grads(info, masks, panels, acts, into=()):
    rows, width = panels[0].shape[0], panels[0].shape[1] // 2
    n = acts.shape[1] // 3 // BLK
    hidden = 2 * n * BLK

    def half(info):
        return (1 - info[0] if into else info[0]) * n

    wide = pl.BlockSpec((width, BLK), lambda j, info, *_: (0, half(info) + j))
    tall = pl.BlockSpec((BLK, width), lambda j, info, *_: (half(info) + j, 0))
    wide_shape = shape((width, hidden), BF)
    return call(
        functools.partial(grads_kernel, mine=not into),
        4,
        (n,),
        [whole(v.shape) for v in panels]
        + [
            pl.BlockSpec((2 * rows, BLK), lambda j, *_, q=q: (0, q * n + j))
            for q in range(3)
        ]
        + [pl.BlockSpec(memory_space=pl.ANY)] * len(into),
        [wide, wide, tall],
        [wide_shape, wide_shape, shape((hidden, width), BF)],
        [pltpu.VMEM((width, 2 * rows), BF), pltpu.VMEM((2 * rows, width), BF)],
        flops=6 * rows * width * hidden,
        size=3 * width * hidden + 6 * rows * hidden,
        **({"input_output_aliases": {9: 0, 10: 1, 11: 2}} if into else {}),
    )(info, *masks, *panels, acts, acts, acts, *into)


def per_device(
    tokens, cotangent, gate_weight, up_weight, down_weight, gate_mask, up_mask, down_mask
):
    masks = (gate_mask, up_mask, down_mask)
    info = lax.dynamic_index_in_dim(jnp.asarray(make_table()), lax.axis_index("col"), 0, keepdims=False)
    both = jnp.concatenate([tokens, cotangent], axis=1)
    x, a, b, ab = (swap_row(both, d) for d in ("X", "A", "B", "AB"))
    gu_own, gu_send, d_own, d_send = prepare(info, *masks, gate_weight, up_weight, down_weight)
    gu_send, d_send, x, a, b, ab = lax.optimization_barrier((gu_send, d_send, x, a, b, ab))
    ax, bx, abx = swap_row(x, "A"), swap_row(x, "B"), swap_row(ab, "X")
    gu_oth, d_oth = swap_core(gu_send), swap_core(d_send)
    own = [jnp.concatenate(blocks, axis=0) for blocks in ([both, x, ax, bx], [abx, ab, a, b])]
    oth = [swap_core(panel) for panel in own]

    panels, weights = (*own, *oth), (gu_own, gu_oth, d_own, d_oth)
    sends = [project(info, panels, weights, 4, (q,), BF)[0] for q in range(3)]
    keeps = project(info, panels, weights, 0, (0, 1, 2), F32)
    acts = gather(info, exchange(sends, keeps))

    got = swap_core(backward(acts, gu_oth, d_oth, F32))
    part = backward(acts, gu_own, d_own, F32) + got
    parts = jnp.split(part, 8, axis=1)
    own_part, x, ax, bx, abx, ab, a, b = parts
    acts, ax, bx, abx, a, b = lax.optimization_barrier([acts] + [v.astype(BF) for v in (ax, bx, abx, a, b)])
    ax, bx, abx = swap_row(ax, "A"), swap_row(bx, "B"), swap_row(abx, "X")
    sib = swap_core(acts)
    partial = grads(info, masks, own, acts)
    x = x + ax.astype(F32) + bx.astype(F32)
    ab = (ab + abx.astype(F32)).astype(BF)
    sib, x, ab, a, b, *partial = lax.optimization_barrier((sib, x, ab, a, b, *partial))
    got = [swap_row(v, d) for v, d in ((ab, "AB"), (x, "X"), (a, "A"), (b, "B"))]
    weight_grads = grads(info, masks, own, sib, partial)
    *weight_grads, got = lax.optimization_barrier((*weight_grads, got))
    total = own_part
    for block in got:
        total = total + block.astype(F32)
    total = total.astype(BF)
    return (total[0], total[1], *weight_grads)


def solution(mesh):
    placed = (
        P("row", "col"),
        P("row", "col"),
        P("col", "row"),
        P("col", "row"),
        P("row", "col"),
        P("col", "row"),
        P("col", "row"),
        P("row", "col"),
    )
    return jax.shard_map(
        per_device,
        mesh=mesh,
        in_specs=placed,
        out_specs=(
            P("row", "col"),
            P("row", "col"),
            P("col", "row"),
            P("col", "row"),
            P("row", "col"),
        ),
        check_vma=False,
    )
```

```python
import functools

import jax
import jax.numpy as jnp
import numpy as np
from jax import lax
from jax.experimental import pallas as pl
from jax.experimental.pallas import tpu as pltpu
from jax.sharding import PartitionSpec as P

BLK = 128
BF = jnp.bfloat16
F32 = jnp.float32

GRAY = ((0, 0), (1, 0), (1, 1), (0, 1))
RING = {bits: pos for pos, bits in enumerate(GRAY)}
MASK = {"A": 4, "B": 2, "X": 1}
ORDERS = ("ABX", "BXA", "XAB")

def flip_ring(pos, dims):
    bit_a, bit_b = GRAY[pos]
    return RING[(bit_a ^ ("A" in dims), bit_b ^ ("B" in dims))]


def flip_col(i, dims):
    z, x, c = i // 4, (i // 2) % 2, i % 2
    return (flip_ring(z, dims) * 2 + (x ^ ("X" in dims))) * 2 + c


def flip_row(i, dims):
    return (i // 4 ^ ("X" in dims)) * 4 + flip_ring(i % 4, dims)


def swap_core(value):
    return lax.ppermute(value, "col", [(i, i ^ 1) for i in range(16)])


def swap_cube(parts, step):
    return [
        lax.ppermute(part, "col", [(i, flip_col(i, order[step])) for i in range(16)])
        for part, order in zip(parts, ORDERS)
    ]


def swap_row(value, dims):
    return lax.ppermute(value, "row", [(i, flip_row(i, dims)) for i in range(8)])


def make_table():
    rows = []
    for i in range(16):
        bit_a, bit_b = GRAY[i // 4]
        own = bit_a * 4 + bit_b * 2 + (i // 2) % 2
        row = [i % 2]
        for order in ORDERS:
            for place in range(8):
                bits = (place >> 2, (place >> 1) & 1, place & 1)
                row.append(own ^ sum(MASK[d] * b for d, b in zip(order, bits)))
        rows.append(row)
    return np.array(rows, np.int32)


def dot(a, b, dims=((1,), (0,))):
    return lax.dot_general(a, b, (dims, ((), ())), preferred_element_type=F32)


NT = ((1,), (1,))
PARAMS = pltpu.CompilerParams(vmem_limit_bytes=24 * 1024 * 1024)


def call(kernel, prefetch, grid, in_specs, out_specs, out_shape, scratch=(), flops=0, size=0, params=PARAMS, **more):
    return pl.pallas_call(
        kernel,
        grid_spec=pltpu.PrefetchScalarGridSpec(
            num_scalar_prefetch=prefetch,
            grid=grid,
            in_specs=in_specs,
            out_specs=out_specs,
            scratch_shapes=list(scratch),
        ),
        out_shape=out_shape,
        compiler_params=params,
        cost_estimate=pl.CostEstimate(flops=flops, bytes_accessed=size, transcendentals=0),
        **more,
    )


def shape(dims, dtype):
    return jax.ShapeDtypeStruct(dims, dtype)


def whole(dims):
    return pl.BlockSpec(dims, lambda *_: (0,) * len(dims))


def times(block, keep):
    return jnp.where(keep != 0, block, jnp.zeros_like(block))


def prepare_kernel(info, gm, um, dm, g, u, d, gu_out, d_out, *, kept):
    f = pl.program_id(0)
    n = g.shape[1] // BLK
    first = (info[0] if kept else 1 - info[0]) * n
    for j in range(n):
        at = slice(j * BLK, (j + 1) * BLK)
        gu_out[0, :, at] = times(g[:, at], gm[f, first + j])
        gu_out[1, :, at] = times(u[:, at], um[f, first + j])
        d_out[at, :] = times(d[at, :], dm[first + j, f])


def prepare(info, masks, gate_weight, up_weight, down_weight, kept):
    width, hidden = gate_weight.shape
    half = hidden // 2

    def side(info):
        return info[0] if kept else 1 - info[0]

    wide = pl.BlockSpec((BLK, half), lambda f, info, *_: (f, side(info)))
    tall = pl.BlockSpec((half, BLK), lambda f, info, *_: (side(info), f))
    return call(
        functools.partial(prepare_kernel, kept=kept),
        4,
        (width // BLK,),
        [wide, wide, tall],
        [
            pl.BlockSpec((2, BLK, half), lambda f, *_: (0, f, 0)),
            pl.BlockSpec((half, BLK), lambda f, *_: (0, f)),
        ],
        [shape((2, width, half), BF), shape((half, width), BF)],
        size=6 * width * hidden,
        params=pltpu.CompilerParams(vmem_limit_bytes=52 * 1024 * 1024),
    )(info, *masks, gate_weight, up_weight, down_weight)


def project_kernel(info, own_a, own_b, oth_a, oth_b, *refs, base, parts):
    outs, panel = refs[-1 - len(parts) : -1], refs[-1]
    rows, width = own_a.shape[0], own_a.shape[1] // 2
    r = rows // 4
    for n, q in enumerate(parts):
        cols = slice(0, width) if q < 2 else slice(width, 2 * width)
        for k in range(4):
            at = info[1 + 8 * q + base + k]
            to = slice(k * r, (k + 1) * r)
            row = pl.ds(pl.multiple_of((at % 4) * r, 16), r)

            @pl.when(at < 4)
            def _():
                panel[n, to, :width] = own_a[row, cols]
                panel[n, to, width:] = oth_a[row, cols]

            @pl.when(at >= 4)
            def _():
                panel[n, to, :width] = own_b[row, cols]
                panel[n, to, width:] = oth_b[row, cols]

    for n, q in enumerate(parts):
        w_own, w_oth = refs[2 * n], refs[2 * n + 1]
        if q < 2:
            w, dims = jnp.concatenate([w_own[0], w_oth[0]], axis=0), ((1,), (0,))
        else:
            w, dims = jnp.concatenate([w_own[...], w_oth[...]], axis=1), NT
        outs[n][...] = dot(panel[n], w, dims).astype(outs[n].dtype)


def project(info, panels, weights, base, parts, kind):
    rows, width = panels[0].shape[0], panels[0].shape[1] // 2
    gu_own, gu_oth, d_own, d_oth = weights
    count = d_own.shape[0]
    args, specs = [], []
    for q in parts:
        if q < 2:
            args += [gu_own, gu_oth]
            specs += [pl.BlockSpec((1, width, count), lambda i, *_, q=q: (q, 0, 0))] * 2
        else:
            args += [d_own, d_oth]
            specs += [whole(d_own.shape)] * 2
    return call(
        functools.partial(project_kernel, base=base, parts=parts),
        1,
        (1,),
        [whole(v.shape) for v in panels] + specs,
        [whole((rows, count))] * len(parts),
        [shape((rows, count), kind)] * len(parts),
        [pltpu.VMEM((len(parts), rows, 2 * width), BF)],
        flops=4 * rows * width * count * len(parts),
        size=4 * (rows + width) * count * len(parts) + 8 * rows * width,
    )(info, *panels, *args)


def pointwise(gate_proj, up_proj, hidden_grad):
    sigmoid_gate = jax.nn.sigmoid(gate_proj)
    silu_gate = gate_proj * sigmoid_gate
    hidden = (silu_gate * up_proj).astype(BF)
    gate_grad = (
        hidden_grad * up_proj * sigmoid_gate * (1.0 + gate_proj * (1.0 - sigmoid_gate))
    ).astype(BF)
    up_grad = (hidden_grad * silu_gate).astype(BF)
    return hidden, gate_grad, up_grad


def exchange(sends, keeps):
    for step in range(3):
        got = swap_cube(sends, step)
        sums = [keep + g.astype(F32) for keep, g in zip(keeps, got)]
        if step < 2:
            n = sums[0].shape[0] // 2
            keeps = [v[:n] for v in sums]
            sends = [v[n:].astype(BF) for v in sums]
    hidden, gate_grad, up_grad = pointwise(*sums)
    parts = [gate_grad, up_grad, hidden]
    for step in (2, 1, 0):
        got = swap_cube(parts, step)
        if step == 0:
            return parts + got
        parts = [jnp.concatenate([part, g], axis=0) for part, g in zip(parts, got)]


def gather_kernel(info, *refs):
    halves, acts = (refs[:3], refs[3:6]), refs[6]
    r = acts.shape[0] // 8
    n = acts.shape[1] // 3
    for q in range(3):
        for k in range(8):
            at = pl.ds(pl.multiple_of(info[1 + 8 * q + k] * r, 16), r)
            acts[at, q * n : (q + 1) * n] = halves[k // 4][q][k % 4 * r : (k % 4 + 1) * r, :]


def gather(info, pieces):
    rows, count = 2 * pieces[0].shape[0], 3 * pieces[0].shape[1]
    return call(
        gather_kernel,
        1,
        (1,),
        [whole(v.shape) for v in pieces],
        whole((rows, count)),
        shape((rows, count), BF),
        size=4 * rows * count,
    )(info, *pieces)


def backward_kernel(acts, gu, d, terms):
    n = acts.shape[1] // 3
    terms[0] = dot(acts[:, 2 * n :], d[...]).astype(terms.dtype)
    inp = dot(acts[:, :n], gu[0], NT) + dot(acts[:, n : 2 * n], gu[1], NT)
    terms[1] = inp.astype(terms.dtype)


def backward(acts, gu, d, kind):
    rows, count, width = acts.shape[0], acts.shape[1], d.shape[1]
    step = 2 * BLK
    return call(
        backward_kernel,
        0,
        (width // step,),
        [
            whole(acts.shape),
            pl.BlockSpec((2, step, d.shape[0]), lambda i: (0, i, 0)),
            pl.BlockSpec((d.shape[0], step), lambda i: (0, i)),
        ],
        pl.BlockSpec((2, rows, step), lambda i: (0, 0, i)),
        shape((2, rows, width), kind),
        flops=2 * rows * width * count,
        size=2 * width * count + 2 * rows * count,
    )(acts, gu, d)


def turn_kernel(own_a, own_b, tok_t, cot):
    rows, width = own_a.shape[0], own_a.shape[1] // 2
    tok_t[:, :rows] = own_a[:, :width].T
    tok_t[:, rows:] = own_b[:, :width].T
    cot[:rows, :] = own_a[:, width:]
    cot[rows:, :] = own_b[:, width:]


def turn(own_a, own_b):
    rows, width = 2 * own_a.shape[0], own_a.shape[1] // 2
    return call(
        turn_kernel,
        0,
        (1,),
        [whole(own_a.shape)] * 2,
        [whole((width, rows)), whole((rows, width))],
        [shape((width, rows), BF), shape((rows, width), BF)],
        size=8 * rows * width,
    )(own_a, own_b)


def grads_kernel(info, gm, um, dm, tok_t, cot, acts, *refs, mine):
    g_out, u_out, d_out = refs[-3:]
    width, count = g_out.shape
    n = count // BLK
    first = (info[0] if mine else 1 - info[0]) * n
    for out, mask, start in ((g_out, gm, 0), (u_out, um, count)):
        grad = dot(tok_t[...], acts[:, start : start + count])
        for f in range(width // BLK):
            for j in range(n):
                at = slice(f * BLK, (f + 1) * BLK), slice(j * BLK, (j + 1) * BLK)
                out[at] = (grad[at] * mask[f, first + j].astype(F32)).astype(BF)
    grad = dot(acts[:, 2 * count :], cot[...], ((0,), (0,)))
    for j in range(n):
        for f in range(width // BLK):
            at = slice(j * BLK, (j + 1) * BLK), slice(f * BLK, (f + 1) * BLK)
            d_out[at] = (grad[at] * dm[first + j, f].astype(F32)).astype(BF)


def grads(info, masks, tok_t, cot, acts, into=()):
    width, rows = tok_t.shape
    count = acts.shape[1] // 3
    hidden = 2 * count

    def half(info):
        return 1 - info[0] if into else info[0]

    wide = pl.BlockSpec((width, count), lambda i, info, *_: (0, half(info)))
    tall = pl.BlockSpec((count, width), lambda i, info, *_: (half(info), 0))
    wide_shape = shape((width, hidden), BF)
    return call(
        functools.partial(grads_kernel, mine=not into),
        4,
        (1,),
        [whole(v.shape) for v in (tok_t, cot, acts)] + [pl.BlockSpec(memory_space=pl.ANY)] * len(into),
        [wide, wide, tall],
        [wide_shape, wide_shape, shape((hidden, width), BF)],
        flops=3 * rows * width * hidden,
        size=3 * width * hidden + 3 * rows * hidden,
        **({"input_output_aliases": {7: 0, 8: 1, 9: 2}} if into else {}),
    )(info, *masks, tok_t, cot, acts, *into)


def per_device(
    tokens, cotangent, gate_weight, up_weight, down_weight, gate_mask, up_mask, down_mask
):
    masks = (gate_mask, up_mask, down_mask)
    info = lax.dynamic_index_in_dim(jnp.asarray(make_table()), lax.axis_index("col"), 0, keepdims=False)
    both = jnp.concatenate([tokens, cotangent], axis=1)
    x, a, b, ab = (swap_row(both, d) for d in ("X", "A", "B", "AB"))
    weights = (gate_weight, up_weight, down_weight)
    gu_send, d_send = prepare(info, masks, *weights, False)
    gu_send, d_send, x, a, b, ab, *weights = lax.optimization_barrier((gu_send, d_send, x, a, b, ab, *weights))
    ax, bx, abx = swap_row(x, "A"), swap_row(x, "B"), swap_row(ab, "X")
    gu_oth, d_oth = swap_core(gu_send), swap_core(d_send)
    gu_own, d_own = prepare(info, masks, *weights, True)
    gu_own, d_own, ax, bx, abx = lax.optimization_barrier((gu_own, d_own, ax, bx, abx))
    own = [jnp.concatenate(blocks, axis=0) for blocks in ([both, x, ax, bx], [abx, ab, a, b])]
    oth = [swap_core(panel) for panel in own]

    panels, weights = (*own, *oth), (gu_own, gu_oth, d_own, d_oth)
    sends = [project(info, panels, weights, 4, (q,), BF)[0] for q in range(3)]
    keeps = project(info, panels, weights, 0, (0, 1, 2), F32)
    tok_t, cot = turn(*own)
    acts = gather(info, exchange(sends, keeps))

    got = swap_core(backward(acts, gu_oth, d_oth, F32))
    part = backward(acts, gu_own, d_own, F32) + got
    parts = jnp.split(part, 8, axis=1)
    own_part, x, ax, bx, abx, ab, a, b = parts
    acts, ax, bx, abx, a, b = lax.optimization_barrier([acts] + [v.astype(BF) for v in (ax, bx, abx, a, b)])
    ax, bx, abx = swap_row(ax, "A"), swap_row(bx, "B"), swap_row(abx, "X")
    sib = swap_core(acts)
    partial = grads(info, masks, tok_t, cot, acts)
    x = x + ax.astype(F32) + bx.astype(F32)
    ab = (ab + abx.astype(F32)).astype(BF)
    sib, x, ab, a, b, *partial = lax.optimization_barrier((sib, x, ab, a, b, *partial))
    got = [swap_row(v, d) for v, d in ((ab, "AB"), (x, "X"), (a, "A"), (b, "B"))]
    weight_grads = grads(info, masks, tok_t, cot, sib, partial)
    *weight_grads, got = lax.optimization_barrier((*weight_grads, got))
    total = own_part
    for block in got:
        total = total + block.astype(F32)
    total = total.astype(BF)
    return (total[0], total[1], *weight_grads)


def solution(mesh):
    placed = (
        P("row", "col"),
        P("row", "col"),
        P("col", "row"),
        P("col", "row"),
        P("row", "col"),
        P("col", "row"),
        P("col", "row"),
        P("row", "col"),
    )
    return jax.shard_map(
        per_device,
        mesh=mesh,
        in_specs=placed,
        out_specs=(
            P("row", "col"),
            P("row", "col"),
            P("col", "row"),
            P("col", "row"),
            P("row", "col"),
        ),
        check_vma=False,
    )
```

```python
import functools

import jax
import jax.numpy as jnp
import numpy as np
from jax import lax
from jax.experimental import pallas as pl
from jax.experimental.pallas import tpu as pltpu
from jax.sharding import PartitionSpec as P

BLK = 128
BF = jnp.bfloat16
F32 = jnp.float32

GRAY = ((0, 0), (1, 0), (1, 1), (0, 1))
RING = {bits: pos for pos, bits in enumerate(GRAY)}
MASK = {"A": 4, "B": 2, "X": 1}
ORDERS = ("ABX", "BXA", "XAB")

def flip_ring(pos, dims):
    bit_a, bit_b = GRAY[pos]
    return RING[(bit_a ^ ("A" in dims), bit_b ^ ("B" in dims))]


def flip_col(i, dims):
    z, x, c = i // 4, (i // 2) % 2, i % 2
    return (flip_ring(z, dims) * 2 + (x ^ ("X" in dims))) * 2 + c


def flip_row(i, dims):
    return (i // 4 ^ ("X" in dims)) * 4 + flip_ring(i % 4, dims)


def swap_core(value):
    return lax.ppermute(value, "col", [(i, i ^ 1) for i in range(16)])


def swap_cube(parts, step):
    return [
        lax.ppermute(part, "col", [(i, flip_col(i, order[step])) for i in range(16)])
        for part, order in zip(parts, ORDERS)
    ]


def swap_row(value, dims):
    return lax.ppermute(value, "row", [(i, flip_row(i, dims)) for i in range(8)])


def make_table():
    rows = []
    for i in range(16):
        bit_a, bit_b = GRAY[i // 4]
        own = bit_a * 4 + bit_b * 2 + (i // 2) % 2
        row = [i % 2]
        for order in ORDERS:
            for place in range(8):
                bits = (place >> 2, (place >> 1) & 1, place & 1)
                row.append(own ^ sum(MASK[d] * b for d, b in zip(order, bits)))
        rows.append(row)
    return np.array(rows, np.int32)


def dot(a, b, dims=((1,), (0,))):
    return lax.dot_general(a, b, (dims, ((), ())), preferred_element_type=F32)


NT = ((1,), (1,))
PARAMS = pltpu.CompilerParams(vmem_limit_bytes=24 * 1024 * 1024)


def call(kernel, prefetch, grid, in_specs, out_specs, out_shape, scratch=(), flops=0, size=0, params=PARAMS, **more):
    return pl.pallas_call(
        kernel,
        grid_spec=pltpu.PrefetchScalarGridSpec(
            num_scalar_prefetch=prefetch,
            grid=grid,
            in_specs=in_specs,
            out_specs=out_specs,
            scratch_shapes=list(scratch),
        ),
        out_shape=out_shape,
        compiler_params=params,
        cost_estimate=pl.CostEstimate(flops=flops, bytes_accessed=size, transcendentals=0),
        **more,
    )


def shape(dims, dtype):
    return jax.ShapeDtypeStruct(dims, dtype)


def whole(dims):
    return pl.BlockSpec(dims, lambda *_: (0,) * len(dims))


def times(block, keep):
    return jnp.where(keep != 0, block, jnp.zeros_like(block))


def prepare_kernel(info, gm, um, dm, g, u, d, gu_out, d_out, *, kept):
    rows, n = g.shape[0] // BLK, g.shape[1] // BLK
    first = (info[0] if kept else 1 - info[0]) * n
    for k in range(rows):
        f = pl.program_id(0) * rows + k
        of = slice(k * BLK, (k + 1) * BLK)
        for j in range(n):
            at = slice(j * BLK, (j + 1) * BLK)
            gu_out[0, of, at] = times(g[of, at], gm[f, first + j])
            gu_out[1, of, at] = times(u[of, at], um[f, first + j])
            d_out[at, of] = times(d[at, of], dm[first + j, f])


def prepare(info, masks, gate_weight, up_weight, down_weight, kept):
    width, hidden = gate_weight.shape
    half = hidden // 2

    def side(info):
        return info[0] if kept else 1 - info[0]

    step = 2 * BLK
    wide = pl.BlockSpec((step, half), lambda f, info, *_: (f, side(info)))
    tall = pl.BlockSpec((half, step), lambda f, info, *_: (side(info), f))
    return call(
        functools.partial(prepare_kernel, kept=kept),
        4,
        (width // step,),
        [wide, wide, tall],
        [
            pl.BlockSpec((2, step, half), lambda f, *_: (0, f, 0)),
            pl.BlockSpec((half, step), lambda f, *_: (0, f)),
        ],
        [shape((2, width, half), BF), shape((half, width), BF)],
        size=6 * width * hidden,
        params=pltpu.CompilerParams(vmem_limit_bytes=52 * 1024 * 1024),
    )(info, *masks, gate_weight, up_weight, down_weight)


def project_kernel(info, own_a, own_b, oth_a, oth_b, *refs, base, parts):
    outs, panel = refs[-1 - len(parts) : -1], refs[-1]
    rows, width = own_a.shape[0], own_a.shape[1] // 2
    r = rows // 4
    for n, q in enumerate(parts):
        cols = slice(0, width) if q < 2 else slice(width, 2 * width)
        for k in range(4):
            at = info[1 + 8 * q + base + k]
            to = slice(k * r, (k + 1) * r)
            row = pl.ds(pl.multiple_of((at % 4) * r, 16), r)

            @pl.when(at < 4)
            def _():
                panel[n, to, :width] = own_a[row, cols]
                panel[n, to, width:] = oth_a[row, cols]

            @pl.when(at >= 4)
            def _():
                panel[n, to, :width] = own_b[row, cols]
                panel[n, to, width:] = oth_b[row, cols]

    for n, q in enumerate(parts):
        w_own, w_oth = refs[2 * n], refs[2 * n + 1]
        if q < 2:
            w, dims = jnp.concatenate([w_own[0], w_oth[0]], axis=0), ((1,), (0,))
        else:
            w, dims = jnp.concatenate([w_own[...], w_oth[...]], axis=1), NT
        outs[n][...] = dot(panel[n], w, dims).astype(outs[n].dtype)


def project(info, panels, weights, base, parts, kind):
    rows, width = panels[0].shape[0], panels[0].shape[1] // 2
    gu_own, gu_oth, d_own, d_oth = weights
    count = d_own.shape[0]
    args, specs = [], []
    for q in parts:
        if q < 2:
            args += [gu_own, gu_oth]
            specs += [pl.BlockSpec((1, width, count), lambda i, *_, q=q: (q, 0, 0))] * 2
        else:
            args += [d_own, d_oth]
            specs += [whole(d_own.shape)] * 2
    return call(
        functools.partial(project_kernel, base=base, parts=parts),
        1,
        (1,),
        [whole(v.shape) for v in panels] + specs,
        [whole((rows, count))] * len(parts),
        [shape((rows, count), kind)] * len(parts),
        [pltpu.VMEM((len(parts), rows, 2 * width), BF)],
        flops=4 * rows * width * count * len(parts),
        size=4 * (rows + width) * count * len(parts) + 8 * rows * width,
    )(info, *panels, *args)


def pointwise(gate_proj, up_proj, hidden_grad):
    sigmoid_gate = jax.nn.sigmoid(gate_proj)
    silu_gate = gate_proj * sigmoid_gate
    hidden = (silu_gate * up_proj).astype(BF)
    gate_grad = (
        hidden_grad * up_proj * sigmoid_gate * (1.0 + gate_proj * (1.0 - sigmoid_gate))
    ).astype(BF)
    up_grad = (hidden_grad * silu_gate).astype(BF)
    return hidden, gate_grad, up_grad


def exchange(sends, keeps):
    for step in range(3):
        got = swap_cube(sends, step)
        sums = [keep + g.astype(F32) for keep, g in zip(keeps, got)]
        if step < 2:
            n = sums[0].shape[0] // 2
            keeps = [v[:n] for v in sums]
            sends = [v[n:].astype(BF) for v in sums]
    hidden, gate_grad, up_grad = pointwise(*sums)
    parts = [gate_grad, up_grad, hidden]
    for step in (2, 1, 0):
        got = swap_cube(parts, step)
        if step == 0:
            return parts + got
        parts = [jnp.concatenate([part, g], axis=0) for part, g in zip(parts, got)]


def gather_kernel(info, *refs):
    halves, acts = (refs[:3], refs[3:6]), refs[6]
    r = acts.shape[0] // 8
    n = acts.shape[1] // 3
    for q in range(3):
        for k in range(8):
            at = pl.ds(pl.multiple_of(info[1 + 8 * q + k] * r, 16), r)
            acts[at, q * n : (q + 1) * n] = halves[k // 4][q][k % 4 * r : (k % 4 + 1) * r, :]


def gather(info, pieces):
    rows, count = 2 * pieces[0].shape[0], 3 * pieces[0].shape[1]
    return call(
        gather_kernel,
        1,
        (1,),
        [whole(v.shape) for v in pieces],
        whole((rows, count)),
        shape((rows, count), BF),
        size=4 * rows * count,
    )(info, *pieces)


def backward_kernel(acts, gu, d, terms):
    n = acts.shape[1] // 3
    terms[0] = dot(acts[:, 2 * n :], d[...]).astype(terms.dtype)
    inp = dot(acts[:, :n], gu[0], NT) + dot(acts[:, n : 2 * n], gu[1], NT)
    terms[1] = inp.astype(terms.dtype)


def backward(acts, gu, d, kind):
    rows, count, width = acts.shape[0], acts.shape[1], d.shape[1]
    step = 2 * BLK
    return call(
        backward_kernel,
        0,
        (width // step,),
        [
            whole(acts.shape),
            pl.BlockSpec((2, step, d.shape[0]), lambda i: (0, i, 0)),
            pl.BlockSpec((d.shape[0], step), lambda i: (0, i)),
        ],
        pl.BlockSpec((2, rows, step), lambda i: (0, 0, i)),
        shape((2, rows, width), kind),
        flops=2 * rows * width * count,
        size=2 * width * count + 2 * rows * count,
    )(acts, gu, d)


def turn_kernel(own_a, own_b, tok_t, cot):
    rows, width = own_a.shape[0], own_a.shape[1] // 2
    tok_t[:, :rows] = own_a[:, :width].T
    tok_t[:, rows:] = own_b[:, :width].T
    cot[:rows, :] = own_a[:, width:]
    cot[rows:, :] = own_b[:, width:]


def turn(own_a, own_b):
    rows, width = 2 * own_a.shape[0], own_a.shape[1] // 2
    return call(
        turn_kernel,
        0,
        (1,),
        [whole(own_a.shape)] * 2,
        [whole((width, rows)), whole((rows, width))],
        [shape((width, rows), BF), shape((rows, width), BF)],
        size=8 * rows * width,
    )(own_a, own_b)


def grads_kernel(info, gm, um, dm, tok_t, cot, acts, *refs, mine):
    g_out, u_out, d_out = refs[-3:]
    width, count = g_out.shape
    n = count // BLK
    first = (info[0] if mine else 1 - info[0]) * n
    for out, mask, start in ((g_out, gm, 0), (u_out, um, count)):
        grad = dot(tok_t[...], acts[:, start : start + count])
        for f in range(width // BLK):
            for j in range(n):
                at = slice(f * BLK, (f + 1) * BLK), slice(j * BLK, (j + 1) * BLK)
                out[at] = (grad[at] * mask[f, first + j].astype(F32)).astype(BF)
    grad = dot(acts[:, 2 * count :], cot[...], ((0,), (0,)))
    for j in range(n):
        for f in range(width // BLK):
            at = slice(j * BLK, (j + 1) * BLK), slice(f * BLK, (f + 1) * BLK)
            d_out[at] = (grad[at] * dm[first + j, f].astype(F32)).astype(BF)


def grads(info, masks, tok_t, cot, acts, into=()):
    width, rows = tok_t.shape
    count = acts.shape[1] // 3
    hidden = 2 * count

    def half(info):
        return 1 - info[0] if into else info[0]

    wide = pl.BlockSpec((width, count), lambda i, info, *_: (0, half(info)))
    tall = pl.BlockSpec((count, width), lambda i, info, *_: (half(info), 0))
    wide_shape = shape((width, hidden), BF)
    return call(
        functools.partial(grads_kernel, mine=not into),
        4,
        (1,),
        [whole(v.shape) for v in (tok_t, cot, acts)] + [pl.BlockSpec(memory_space=pl.ANY)] * len(into),
        [wide, wide, tall],
        [wide_shape, wide_shape, shape((hidden, width), BF)],
        flops=3 * rows * width * hidden,
        size=3 * width * hidden + 3 * rows * hidden,
        **({"input_output_aliases": {7: 0, 8: 1, 9: 2}} if into else {}),
    )(info, *masks, tok_t, cot, acts, *into)


def per_device(
    tokens, cotangent, gate_weight, up_weight, down_weight, gate_mask, up_mask, down_mask
):
    masks = (gate_mask, up_mask, down_mask)
    info = lax.dynamic_index_in_dim(jnp.asarray(make_table()), lax.axis_index("col"), 0, keepdims=False)
    both = jnp.concatenate([tokens, cotangent], axis=1)
    a, b, x, ab = (swap_row(both, d) for d in ("A", "B", "X", "AB"))
    weights = (gate_weight, up_weight, down_weight)
    gu_send, d_send = prepare(info, masks, *weights, False)
    gu_send, d_send, a, b, x, ab, *weights = lax.optimization_barrier((gu_send, d_send, a, b, x, ab, *weights))
    ax, bx, abx = swap_row(x, "A"), swap_row(x, "B"), swap_row(ab, "X")
    gu_oth, d_oth = swap_core(gu_send), swap_core(d_send)
    gu_own, d_own = prepare(info, masks, *weights, True)
    gu_own, d_own, ax, bx, abx = lax.optimization_barrier((gu_own, d_own, ax, bx, abx))
    own = [jnp.concatenate(blocks, axis=0) for blocks in ([both, x, ax, bx], [abx, ab, a, b])]
    oth = [swap_core(panel) for panel in own]

    panels, weights = (*own, *oth), (gu_own, gu_oth, d_own, d_oth)
    sends = [project(info, panels, weights, 4, (q,), BF)[0] for q in range(3)]
    keeps = project(info, panels, weights, 0, (0, 1, 2), F32)
    tok_t, cot = turn(*own)
    acts = gather(info, exchange(sends, keeps))

    got = swap_core(backward(acts, gu_oth, d_oth, F32))
    part = backward(acts, gu_own, d_own, F32) + got
    parts = jnp.split(part, 8, axis=1)
    own_part, x, ax, bx, abx, ab, a, b = parts
    acts, ax, bx, abx, a, b = lax.optimization_barrier([acts] + [v.astype(BF) for v in (ax, bx, abx, a, b)])
    ax, bx, abx = swap_row(ax, "A"), swap_row(bx, "B"), swap_row(abx, "X")
    sib = swap_core(acts)
    partial = grads(info, masks, tok_t, cot, acts)
    x = x + ax.astype(F32) + bx.astype(F32)
    ab = (ab + abx.astype(F32)).astype(BF)
    sib, x, ab, a, b, *partial = lax.optimization_barrier((sib, x, ab, a, b, *partial))
    got = [swap_row(v, d) for v, d in ((ab, "AB"), (x, "X"), (a, "A"), (b, "B"))]
    weight_grads = grads(info, masks, tok_t, cot, sib, partial)
    *weight_grads, got = lax.optimization_barrier((*weight_grads, got))
    total = own_part
    for block in got:
        total = total + block.astype(F32)
    total = total.astype(BF)
    return (total[0], total[1], *weight_grads)


def solution(mesh):
    placed = (
        P("row", "col"),
        P("row", "col"),
        P("col", "row"),
        P("col", "row"),
        P("row", "col"),
        P("col", "row"),
        P("col", "row"),
        P("row", "col"),
    )
    return jax.shard_map(
        per_device,
        mesh=mesh,
        in_specs=placed,
        out_specs=(
            P("row", "col"),
            P("row", "col"),
            P("col", "row"),
            P("col", "row"),
            P("row", "col"),
        ),
        check_vma=False,
    )
```
